32 devices in a mesh: groups: 2 (over x), wide: 16 (over z, y, core).
Axes of the slice: x: 2, y: 2, z: 4, core: 2. Of those that a mesh axis runs over, the one named last changes fastest.
Arguments:
- gen_cost: float32 [3072, 64], P(('groups', 'wide')), parts along dimension 0, may hold values from -6 to 6
- demand: float32 [20480, 64], P(('groups', 'wide')), parts along dimension 0, may hold values from -4 to 4
- ptdf_rows: bfloat16 [10240, 2048], P('wide'), may hold values from -0.15625 to 0.15625
- gen_zone: int32 [1536, 1], P('wide'), may hold values from 0 to 15; in each aligned block of 96 rows (0 to 95, 96 to 191, ...) at most 12 rows name the same one
- gen_local: int32 [1536], P('wide'), may hold values from 0 to 639
- gen_max: float32 [1536], P('wide'), may hold values from 0.3 to 3
- ramp_limit: float32 [1536], P('wide'), may hold values from 0.02 to 0.5
- line_limit: float32 [2048], replicated, may hold values from 0.1 to 1.5
- primal_start: float32 [3072, 64], P(('groups', 'wide')), parts along dimension 0, may hold values from 0 to 1
- balance_start: float32 [20480, 64], P(('groups', 'wide')), parts along dimension 0, may hold values from -4 to 4
- flow_start: float32 [128, 2048], P(('groups', 'wide')), parts along dimension 0, may hold values from -4 to 4
- ramp_start: float32 [3072, 64], P(('groups', 'wide')), parts along dimension 0, may hold values from -4 to 4
Outputs:
- primal: float32 [3072, 64], P(('groups', 'wide')), parts along dimension 0
- balance_dual: float32 [20480, 64], P(('groups', 'wide')), parts along dimension 0
- flow_dual: float32 [128, 2048], P(('groups', 'wide')), parts along dimension 0
- ramp_dual: float32 [3072, 64], P(('groups', 'wide')), parts along dimension 0
The draws below stay inside these ranges and needn't reach their ends.
There are 2 independent parts, one for each index of `groups`. The reference program is written for one: setup_inputs(seed, part) draws one part's arguments, and reference() takes and returns one part's arrays. A program takes and returns all parts, laid end to end along the dimension named above; an argument that names none is the same for every part. Nothing has to cross between parts.
Inputs may be any that keep to these rules, and one draw needn't show every extreme that they name: `gen_zone`: among the 96 generators of one device (aligned blocks) at most 12 connect to one zone, and exactly 12 to some zone in some block.
All inputs are finite; a program needn't handle non-finite values.
Results may differ from the reference program's by a relative error of at most 0.0015.
Values may be sent and summed in bfloat16 or wider, within the bound.
A program may use at most 64 MiB of HBM per device.

```python
import math
import jax
import jax.numpy as jnp
import numpy as np

GEN_DEV = 96
BUS_DEV = 640
LINES = 2048
ITERS = 3
GENS = 1536
BUSES = 10240
HOURS = 64
CAP = 12
N_WIDE = 16


def plant(entries, rng, least, high):
    place = [jax.random.randint(jax.random.fold_in(rng, axis), (), 0, length) for axis, length in enumerate(entries.shape)]
    widest = entries.shape.index(max(entries.shape))
    beside = place[:widest] + [(place[widest] + 1) % entries.shape[widest]] + place[widest + 1:]
    return entries.at[tuple(place)].set(least).at[tuple(beside)].set(high)


def shard_levels(rng, extent, shards, least, largest):
    gain = 1.0
    for dim, parts in shards:
        draws = jax.random.uniform(jax.random.fold_in(jax.random.fold_in(rng, 6), dim), (parts,), jnp.float32, least / len(shards), largest / len(shards))
        gain = gain * jnp.repeat(jnp.exp(draws), extent[dim] // parts).reshape((-1,) + (1,) * (len(extent) - 1 - dim))
    return gain


def routed_block(rng, own, number, rows, amount, top, limit, lean):
    order = jax.random.permutation(rng, amount)
    packed, common = portions_of(amount, rows * top, limit, lean, True), portions_of(amount, rows * top, limit, lean, False)
    places = jnp.arange(amount)

    def named(sizes, offset_by):
        used = int((sizes > 0).sum())
        fixed = max(1, used // 4)
        moved = fixed + (places - fixed + offset_by * (used - fixed)) % max(1, amount - fixed)
        return jnp.zeros((amount,), jnp.int32).at[order[jnp.where(places < fixed, places, moved)]].set(jnp.asarray(sizes, jnp.int32))

    sizes = jnp.where(number % 4 == 0, named(packed, number // 4), named(common, number - number // 4 - 1))
    mixed = jax.random.permutation(jax.random.fold_in(own, 3), amount)
    source_of, receiver = mixed[0:amount // 2 * 2:2], mixed[1:amount // 2 * 2:2]
    room = jnp.minimum(sizes[source_of] - 1, limit - sizes[receiver]) // 2
    room = jnp.where((source_of == order[0]) | (receiver == order[0]) | (sizes[receiver] == 0), 0, jnp.maximum(room, 0))
    moved = jax.random.randint(jax.random.fold_in(own, 4), (amount // 2,), 0, 1 << 20) % (room + 1)
    sizes = sizes.at[source_of].add(-moved).at[receiver].add(moved)
    members = jnp.searchsorted(jnp.cumsum(sizes), jnp.arange(rows * top), side="right").astype(jnp.int32)
    grid = members.reshape(top, rows).T
    grid = grid[jax.random.permutation(jax.random.fold_in(own, 1), rows)]
    offset_by = jax.random.randint(jax.random.fold_in(own, 2), (rows, 1), 0, top)
    return jnp.take_along_axis(grid, (jnp.arange(top)[None, :] + offset_by) % top, axis=1)


def portions_of(number_of, total, limit, lean, full):
    weights = [(1 << 20) // math.isqrt(standing ** lean) + 1 for standing in range(1, number_of + 1)]
    largest = limit if full else min(limit, max(-(-total // number_of), total * weights[0] // sum(weights)))
    least = 1 if total - largest >= number_of - 1 else 0
    holding, rest = [largest] + [least] * (number_of - 1), total - largest - least * (number_of - 1)
    while rest > 0:
        movable = [i for i in range(1, number_of) if holding[i] < largest] or [i for i in range(1, number_of) if holding[i] < limit]
        whole, left = sum([weights[i] for i in movable]), rest
        for i in movable:
            more = min(limit - holding[i], max(1, left * weights[i] // whole), rest)
            holding[i] = holding[i] + more
            rest = rest - more
    return np.array(holding)


def noise(own_key, shape, scale, bound, cuts=(), held_as=jnp.bfloat16):
    factor_of = shard_levels(own_key, shape, cuts, -0.22, 0.18) if cuts else 1.0
    values = jax.random.normal(own_key, shape, jnp.float32) * scale * factor_of
    return jnp.minimum(jnp.maximum(values, -bound), bound).astype(held_as)


def setup_inputs(seed: int = 0, part: int = 0) -> dict:
    key_list = jax.random.split(jax.random.key(seed), 13)
    own_keys = jax.random.split(jax.random.fold_in(key_list[12], part), 13)
    gen_cost = noise(own_keys[0], (GENS, HOURS), 1.0, 6.0, ((0, 16),), jnp.float32)
    demand = noise(own_keys[1], (BUSES, HOURS), 0.5, 4.0, ((0, 16),), jnp.float32)
    ptdf_rows = noise(key_list[2], (BUSES, LINES), GENS ** -0.5, 0.15625, ((0, 16),))
    gen_zone_keys = jax.random.split(jax.random.fold_in(key_list[3], 1), GENS // GEN_DEV)
    gen_zone_turns = jax.random.permutation(jax.random.fold_in(key_list[3], 3), GENS // GEN_DEV)
    gen_zone = jax.vmap(lambda own, number: routed_block(jax.random.fold_in(key_list[3], 2), own, number, GEN_DEV, N_WIDE, 1, CAP, 2))(gen_zone_keys, gen_zone_turns).reshape((GENS, 1))
    gen_local = plant(jax.random.randint(key_list[4], (GENS,), 0, BUS_DEV), jax.random.fold_in(key_list[4], 1), 0, BUS_DEV - 1).astype(jnp.int32)
    gen_max = jnp.clip(jnp.exp(math.log(3.0) - 2.3025851 * jax.random.uniform(key_list[5], (GENS,), jnp.float32) ** shard_levels(key_list[5], (GENS,), ((0, 16),), -0.2, 0.2)), 0.3, 3.0)
    ramp_limit = jnp.clip(jnp.exp(math.log(0.5) - 3.218876 * jax.random.uniform(key_list[6], (GENS,), jnp.float32) ** shard_levels(key_list[6], (GENS,), ((0, 16),), -0.2, 0.2)), 0.02, 0.5)
    line_limit = jnp.clip(jnp.exp(jax.random.uniform(key_list[7], (LINES,), jnp.float32, math.log(0.1), math.log(1.5))), 0.1, 1.5)
    primal_start = jnp.clip(1.0 * jax.random.uniform(own_keys[8], (GENS, HOURS), jnp.float32) ** shard_levels(own_keys[8], (GENS, HOURS), ((0, 16),), -0.2, 0.2), 0.0, 1.0)
    balance_start = noise(own_keys[9], (BUSES, HOURS), 0.5, 4.0, ((0, 16),), jnp.float32)
    flow_start = noise(own_keys[10], (HOURS, LINES), 0.5, 4.0, ((0, 16),), jnp.float32)
    ramp_start = noise(own_keys[11], (GENS, HOURS), 0.5, 4.0, ((0, 16),), jnp.float32)
    return {"gen_cost": gen_cost, "demand": demand, "ptdf_rows": ptdf_rows, "gen_zone": gen_zone, "gen_local": gen_local, "gen_max": gen_max, "ramp_limit": ramp_limit, "line_limit": line_limit, "primal_start": primal_start, "balance_start": balance_start, "flow_start": flow_start, "ramp_start": ramp_start}


step_primal = 0.25
step_dual = 0.25


def ramp_image(field):
    shifted = jnp.concatenate([field[:, :1], field[:, :-1]], axis=1)
    return field - shifted


def ramp_adjoint(dual):
    column = jnp.arange(dual.shape[1])[None, :]
    masked = jnp.where(column > 0, dual, jnp.float32(0.0))
    following = jnp.concatenate([masked[:, 1:], jnp.zeros_like(masked[:, :1])], axis=1)
    return masked - following


def reference(gen_cost, demand, ptdf_rows, gen_zone, gen_local, gen_max, ramp_limit, line_limit, primal_start, balance_start, flow_start, ramp_start):
    bus_index = (gen_zone[:, 0] * BUS_DEV + gen_local).astype(jnp.int32)
    primal = primal_start
    balance = balance_start
    flow_dual = flow_start
    ramp_dual = ramp_start
    for iteration in range(ITERS):
        flow_half = flow_dual.astype(jnp.bfloat16)
        bus_dual = balance + jnp.dot(ptdf_rows, flow_half.T, preferred_element_type=jnp.float32)
        gen_dual = bus_dual[bus_index]
        moved = primal - step_primal * (gen_cost + gen_dual + ramp_adjoint(ramp_dual))
        primal_new = jnp.clip(moved, 0.0, gen_max[:, None])
        extra = 2.0 * primal_new - primal
        injection = jax.ops.segment_sum(extra, bus_index, num_segments=BUSES)
        balance = balance + step_dual * (injection - demand)
        inj_half = injection.astype(jnp.bfloat16)
        flows = jnp.dot(inj_half.T, ptdf_rows, preferred_element_type=jnp.float32)
        value = flow_dual + step_dual * flows
        flow_dual = value - step_dual * jnp.clip(value / step_dual, -line_limit[None, :], line_limit[None, :])
        ramp_value = ramp_dual + step_dual * ramp_image(extra)
        ramp_dual = ramp_value - step_dual * jnp.clip(ramp_value / step_dual, -ramp_limit[:, None], ramp_limit[:, None])
        primal = primal_new
    return primal, balance, flow_dual, ramp_dual
```

```python
import functools

import jax
import jax.numpy as jnp
from jax import lax
from jax.experimental import pallas as pl
from jax.experimental.pallas import tpu as pltpu
from jax.sharding import PartitionSpec as P

ITERS = 3
STEP = 0.25
F32 = jnp.float32
BF16 = jnp.bfloat16
HIGH = lax.Precision.HIGHEST


def dot(a, b, dims=((1,), (0,)), precision=None):
    return lax.dot_general(a, b, (dims, ((), ())), preferred_element_type=F32, precision=precision)


def iota(shape, dim):
    return lax.broadcasted_iota(jnp.int32, shape, dim)


def shrink(value, limit):
    return value - STEP * jnp.clip(value * (1.0 / STEP), -limit, limit)


def kernel(
    n,
    cap,
    cost_ref,
    demand_ref,
    ptdf_hbm,
    zone_ref,
    local_ref,
    gmax_ref,
    rlim_ref,
    llim_ref,
    x_ref,
    yb_ref,
    yf_ref,
    yr_ref,
    x_out,
    yb_out,
    yf_out,
    yr_out,
    ptdf,
    payload,
    packed,
    arrived,
    turned,
    back,
    returned,
    part,
    cbuf,
    sbuf,
    rbuf,
    duals,
    fold_lim,
    fold_yf,
    in_sem,
    a_send,
    a_recv,
    b_send,
    b_recv,
    c_send,
    c_recv,
    r_send,
    r_recv,
    g_send,
    g_recv,
    f_send,
    f_recv,
):
    nc = n // 2
    gens, hours = cost_ref.shape
    buses, lines = ptdf.shape
    hr = yf_ref.shape[0]
    slots = n * cap
    folds = fold_yf.shape[0] // hr
    rows = hr * folds
    span = lines // folds
    me = lax.axis_index("wide")
    core = lax.rem(me, 2)
    chip = me // 2
    partner = chip * 2 + 1 - core

    def other(k):
        return lax.rem(me + k, n)

    def before(k):
        return lax.rem(me + n - k, n)

    def chip_after(k):
        return lax.rem(chip + k, nc)

    def chip_before(k):
        return lax.rem(chip + nc - k, nc)

    def remote(src, dst, send, recv, target):
        return pltpu.make_async_remote_copy(
            src_ref=src,
            dst_ref=dst,
            send_sem=send,
            recv_sem=recv,
            device_id={"wide": target},
            device_id_type=pl.DeviceIdType.MESH,
        )

    def loop(first, last, body):
        def step(k, carry):
            body(k)
            return carry

        lax.fori_loop(first, last, step, 0)

    barrier = pltpu.get_barrier_semaphore()

    def greet(k):
        pl.semaphore_signal(
            barrier, inc=1, device_id={"wide": other(k)}, device_id_type=pl.DeviceIdType.MESH
        )

    loop(1, n, greet)
    load = pltpu.make_async_copy(ptdf_hbm, ptdf, in_sem)
    load.start()

    for q in range(folds):
        cols = slice(q * span, (q + 1) * span)
        fold_yf[q * hr : (q + 1) * hr, :] = yf_ref[:, cols]
        fold_lim[q * hr : (q + 1) * hr, :] = jnp.broadcast_to(llim_ref[:, cols], (hr, span))

    def own_rows(c, ch):
        return pl.ds(pl.multiple_of((c * nc + ch) * rows, rows), rows)

    duals[0, own_rows(core, chip), :] = fold_yf[...].astype(BF16)

    zone = zone_ref[...]
    member = (zone == iota((gens, n), 1)).astype(F32)
    earlier = (iota((gens, gens), 0) > iota((gens, gens), 1)).astype(F32)
    ahead = dot(earlier.astype(BF16), member.astype(BF16))
    rank = jnp.sum(ahead * member, axis=1, keepdims=True).astype(jnp.int32)
    slot_col = zone * cap + rank
    eye = iota((gens, gens), 0) == iota((gens, gens), 1)
    slot_row = jnp.sum(
        jnp.where(eye, jnp.broadcast_to(slot_col.astype(F32), (gens, gens)), 0.0),
        axis=0,
        keepdims=True,
    ).astype(jnp.int32)

    def column(row):
        wide = jnp.broadcast_to(row, (gens, gens))
        return jnp.sum(jnp.where(eye, wide, 0.0), axis=1, keepdims=True)

    payload[...] = jnp.zeros_like(payload)
    payload[:, 0:hours] = cost_ref[...]
    payload[:, hours : 2 * hours] = x_ref[...]
    payload[:, 2 * hours : 3 * hours] = yr_ref[...]
    payload[:, 3 * hours : 3 * hours + 1] = column(gmax_ref[...])
    payload[:, 3 * hours + 1 : 3 * hours + 2] = column(rlim_ref[...])
    payload[:, 3 * hours + 2 : 3 * hours + 3] = column(local_ref[...].astype(F32)) + 1.0
    packing = (iota((slots, gens), 0) == slot_row).astype(F32)
    packed[...] = dot(packing, payload[...], precision=HIGH)

    pl.semaphore_wait(barrier, n - 1)

    def gather(it):
        mine = duals.at[it, own_rows(core, chip)]
        near = remote(mine, mine, f_send.at[it, 0], f_recv.at[it, 0], partner)
        near.start()

        def out(k):
            return remote(
                mine, mine, g_send.at[it, k], g_recv.at[it, k], chip_after(k) * 2 + core
            )

        loop(1, nc, lambda k: out(k).start())

    def gather_end(it):
        def into(k, c):
            return duals.at[it, own_rows(c, chip_before(k))]

        def forward(k):
            got = into(k, core)
            remote(got, got, g_send.at[it, k], g_recv.at[it, k], partner).wait_recv()
            remote(got, got, f_send.at[it, k], f_recv.at[it, k], partner).start()

        loop(1, nc, forward)

        def finish(k):
            got = into(k, 1 - core)
            remote(got, got, f_send.at[it, k], f_recv.at[it, k], partner).wait_recv()

        loop(0, nc, finish)

    def gather_sent(it):
        mine = duals.at[it, own_rows(core, chip)]
        remote(mine, mine, f_send.at[it, 0], f_recv.at[it, 0], partner).wait_send()

        def sent(k):
            remote(mine, mine, g_send.at[it, k], g_recv.at[it, k], partner).wait_send()
            got = duals.at[it, own_rows(core, chip_before(k))]
            remote(got, got, f_send.at[it, k], f_recv.at[it, k], partner).wait_send()

        loop(1, nc, sent)

    def rows_of(w):
        return pl.ds(pl.multiple_of(w * cap, cap), cap)

    def exchange(src, dst, send, recv):
        def go(k):
            remote(
                src.at[rows_of(other(k))], dst.at[rows_of(me)], send.at[k], recv.at[k], other(k)
            ).start()

        loop(1, n, go)
        dst[rows_of(me), :] = src[rows_of(me), :]

    def exchange_end(src, dst, send, recv):
        def end(k):
            remote(
                src.at[rows_of(other(k))],
                dst.at[rows_of(before(k))],
                send.at[k],
                recv.at[k],
                other(k),
            ).wait()

        loop(1, n, end)

    exchange(packed, arrived, a_send, a_recv)
    gather(0)
    exchange_end(packed, arrived, a_send, a_recv)

    ids = arrived[:, 3 * hours + 2 : 3 * hours + 3].astype(jnp.int32)
    turned[...] = arrived[...].T
    cost = turned[0:hours, :]
    x = turned[hours : 2 * hours, :]
    yr = turned[2 * hours : 3 * hours, :]
    gmax = turned[3 * hours : 3 * hours + 1, :]
    rlim = turned[3 * hours + 1 : 3 * hours + 2, :]
    id_row = turned[3 * hours + 2 : 3 * hours + 3, :].astype(jnp.int32)
    at_bus = (iota((slots, buses), 1) + 1 == ids).astype(F32)
    same_bool = (ids == id_row) & (ids > 0)
    same = same_bool.astype(F32)
    repeats = jnp.max(
        jnp.where(iota((slots, slots), 0) < iota((slots, slots), 1), same, 0.0),
        axis=0,
        keepdims=True,
    )
    lead = jnp.where((repeats == 0.0) & (id_row > 0), 1.0, 0.0)
    yb_slot = dot(at_bus, yb_ref[...], precision=HIGH).T
    demand_slot = dot(at_bus, demand_ref[...], precision=HIGH).T
    load.wait()
    at_bus16 = at_bus.astype(BF16)
    rows16 = [
        dot(at_bus16, ptdf[:, q * span : (q + 1) * span]).astype(BF16) for q in range(folds)
    ]

    piece_row = iota((n * rows, hours), 0)
    block = piece_row // rows
    owner = lax.rem(block, nc) * 2 + block // nc
    within = lax.rem(piece_row, rows)
    hour_of = owner * hr + lax.rem(within, hr)
    fold_of = within // hr
    at_hour = hour_of == iota((n * rows, hours), 1)
    spread = [(at_hour & (fold_of == q)).astype(F32).astype(BF16) for q in range(folds)]
    t_row = iota((hours, n * rows), 1)
    t_block = t_row // rows
    t_owner = lax.rem(t_block, nc) * 2 + t_block // nc
    t_within = lax.rem(t_row, rows)
    t_at = (t_owner * hr + lax.rem(t_within, hr)) == iota((hours, n * rows), 0)
    collect = [(t_at & (t_within // hr == q)).astype(F32).astype(BF16) for q in range(folds)]

    hour = iota((hours, slots), 0)
    total = jnp.zeros((hours, slots), F32)
    for it in range(ITERS):
        gather_end(it)
        gen_dual = yb_slot
        for q in range(folds):
            line16 = dot(collect[q], duals[it]).astype(BF16)
            gen_dual = gen_dual + dot(line16, rows16[q], ((1,), (1,)))
        masked = jnp.where(hour > 0, yr, 0.0)
        following = jnp.where(hour < hours - 1, pltpu.roll(masked, hours - 1, 0), 0.0)
        moved = x - STEP * (cost + gen_dual + (masked - following))
        x_new = jnp.clip(moved, 0.0, gmax)
        extra = 2.0 * x_new - x
        injection = dot(extra, same, precision=HIGH)
        inj16 = (injection * lead).astype(BF16)
        mixed = None
        for q in range(folds):
            term = dot(dot(spread[q], inj16).astype(BF16), rows16[q])
            mixed = term if mixed is None else mixed + term
        part[it] = mixed

        def give(k):
            return remote(
                part.at[it, own_rows(1 - core, chip_after(k))],
                cbuf.at[it, k],
                c_send.at[it, k],
                c_recv.at[it, k],
                partner,
            )

        def spoke(k):
            return remote(
                sbuf.at[it, k],
                rbuf.at[it, k],
                r_send.at[it, k],
                r_recv.at[it, k],
                chip_after(k) * 2 + core,
            )

        loop(1, nc, lambda k: give(k).start())
        give(0).start()

        total = total + injection
        yb_slot = yb_slot + STEP * (injection - demand_slot)
        change = jnp.where(hour > 0, extra - pltpu.roll(extra, 1, 0), 0.0)
        yr = shrink(yr + STEP * change, rlim)
        x = x_new

        def pass_on(k):
            give(k).wait_recv()
            sbuf[it, k] = part[it, own_rows(core, chip_after(k)), :] + cbuf[it, k]
            spoke(k).start()

        loop(1, nc, pass_on)
        give(0).wait_recv()
        mine = part[it, own_rows(core, chip), :] + cbuf[it, 0]
        if it == ITERS - 1:
            back[...] = jnp.concatenate([x, yr], axis=0).T
            exchange(back, returned, b_send, b_recv)
            placing = (iota((buses, slots), 0) + 1 == id_row).astype(F32) * lead
            placed = dot(placing, total.T, precision=HIGH)
            yb_out[...] = yb_ref[...] + STEP * (placed - ITERS * demand_ref[...])

        def add(k, acc):
            spoke(k).wait_recv()
            return acc + rbuf[it, k]

        flows = lax.fori_loop(1, nc, add, mine)
        fold_yf[...] = shrink(fold_yf[...] + STEP * flows, fold_lim[...])
        if it < ITERS - 1:
            duals[it + 1, own_rows(core, chip), :] = fold_yf[...].astype(BF16)
            gather(it + 1)

    for q in range(folds):
        yf_out[:, q * span : (q + 1) * span] = fold_yf[q * hr : (q + 1) * hr, :]
    exchange_end(back, returned, b_send, b_recv)
    unpack = (iota((gens, slots), 1) == slot_col).astype(F32)
    result = dot(unpack, returned[...], precision=HIGH)
    x_out[...] = result[:, 0:hours]
    yr_out[...] = result[:, hours : 2 * hours]

    for it in range(ITERS):
        gather_sent(it)

        def done(k):
            remote(
                part.at[it, own_rows(1 - core, chip_after(k))],
                cbuf.at[it, k],
                c_send.at[it, k],
                c_recv.at[it, k],
                partner,
            ).wait_send()

        loop(0, nc, done)

        def done_far(k):
            remote(
                sbuf.at[it, k], rbuf.at[it, k], r_send.at[it, k], r_recv.at[it, k], partner
            ).wait_send()

        loop(1, nc, done_far)


def per_device(
    gen_cost,
    demand,
    ptdf_rows,
    gen_zone,
    gen_local,
    gen_max,
    ramp_limit,
    line_limit,
    primal_start,
    balance_start,
    flow_start,
    ramp_start,
):
    n = lax.axis_size("wide")
    nc = n // 2
    gens, hours = primal_start.shape
    buses, lines = ptdf_rows.shape
    hr = flow_start.shape[0]
    cap = -(-max(2, 2 * gens // n) // 8) * 8
    slots = n * cap
    folds = max(1, 16 // hr)
    rows = hr * folds
    span = lines // folds
    width = -(-(3 * hours + 3) // 128) * 128
    vmem = pl.BlockSpec(memory_space=pltpu.VMEM)
    dma = pltpu.SemaphoreType.DMA
    shape = jax.ShapeDtypeStruct
    return pl.pallas_call(
        functools.partial(kernel, n, cap),
        out_shape=(
            shape(primal_start.shape, F32),
            shape(balance_start.shape, F32),
            shape(flow_start.shape, F32),
            shape(ramp_start.shape, F32),
        ),
        in_specs=[vmem, vmem, pl.BlockSpec(memory_space=pl.ANY)] + [vmem] * 9,
        out_specs=(vmem,) * 4,
        scratch_shapes=[
            pltpu.VMEM((buses, lines), BF16),
            pltpu.VMEM((gens, width), F32),
            pltpu.VMEM((slots, width), F32),
            pltpu.VMEM((slots, width), F32),
            pltpu.VMEM((width, slots), F32),
            pltpu.VMEM((slots, 2 * hours), F32),
            pltpu.VMEM((slots, 2 * hours), F32),
            pltpu.VMEM((ITERS, n * rows, span), F32),
            pltpu.VMEM((ITERS, nc, rows, span), F32),
            pltpu.VMEM((ITERS, nc, rows, span), F32),
            pltpu.VMEM((ITERS, nc, rows, span), F32),
            pltpu.VMEM((ITERS, n * rows, span), BF16),
            pltpu.VMEM((rows, span), F32),
            pltpu.VMEM((rows, span), F32),
            dma(()),
            dma((n,)),
            dma((n,)),
            dma((n,)),
            dma((n,)),
        ]
        + [dma((ITERS, nc))] * 8,
        compiler_params=pltpu.CompilerParams(
            collective_id=0, has_side_effects=True, vmem_limit_bytes=56 * 1024 * 1024
        ),
    )(
        gen_cost,
        demand,
        ptdf_rows,
        gen_zone,
        gen_local.reshape(1, gens),
        gen_max.reshape(1, gens),
        ramp_limit.reshape(1, gens),
        line_limit.reshape(1, lines),
        primal_start,
        balance_start,
        flow_start,
        ramp_start,
    )


def solution(mesh):
    both = P(("groups", "wide"), None)
    placed = (
        both,
        both,
        P("wide", None),
        P("wide", None),
        P("wide"),
        P("wide"),
        P("wide"),
        P(),
        both,
        both,
        both,
        both,
    )
    return jax.shard_map(
        per_device, mesh=mesh, in_specs=placed, out_specs=(both,) * 4, check_vma=False
    )
```

```python
import functools

import jax
import jax.numpy as jnp
from jax import lax
from jax.experimental import pallas as pl
from jax.experimental.pallas import tpu as pltpu
from jax.sharding import PartitionSpec as P

ITERS = 3
STEP = 0.25
F32 = jnp.float32
BF16 = jnp.bfloat16
HIGH = lax.Precision.HIGHEST


def dot(a, b, dims=((1,), (0,)), precision=None):
    return lax.dot_general(a, b, (dims, ((), ())), preferred_element_type=F32, precision=precision)


def iota(shape, dim):
    return lax.broadcasted_iota(jnp.int32, shape, dim)


def shrink(value, limit):
    return value - STEP * jnp.clip(value * (1.0 / STEP), -limit, limit)


def kernel(
    n,
    cap,
    cost_ref,
    demand_ref,
    ptdf_hbm,
    zone_ref,
    local_ref,
    gmax_ref,
    rlim_ref,
    llim_ref,
    x_ref,
    yb_ref,
    yf_ref,
    yr_ref,
    x_out,
    yb_out,
    yf_out,
    yr_out,
    ptdf,
    payload,
    packed,
    arrived,
    turned,
    back,
    returned,
    part,
    cbuf,
    sbuf,
    rbuf,
    duals,
    fold_lim,
    fold_yf,
    in_sem,
    a_send,
    a_recv,
    b_send,
    b_recv,
    c_send,
    c_recv,
    r_send,
    r_recv,
    g_send,
    g_recv,
    f_send,
    f_recv,
):
    nc = n // 2
    hours, gens = cost_ref.shape
    buses, lines = ptdf.shape
    hr = yf_ref.shape[0]
    slots = n * cap
    folds = fold_yf.shape[0] // hr
    rows = hr * folds
    span = lines // folds
    me = lax.axis_index("wide")
    core = lax.rem(me, 2)
    chip = me // 2
    partner = chip * 2 + 1 - core

    def other(k):
        return lax.rem(me + k, n)

    def before(k):
        return lax.rem(me + n - k, n)

    def chip_after(k):
        return lax.rem(chip + k, nc)

    def chip_before(k):
        return lax.rem(chip + nc - k, nc)

    def remote(src, dst, send, recv, target):
        return pltpu.make_async_remote_copy(
            src_ref=src,
            dst_ref=dst,
            send_sem=send,
            recv_sem=recv,
            device_id={"wide": target},
            device_id_type=pl.DeviceIdType.MESH,
        )

    def loop(first, last, body):
        def step(k, carry):
            body(k)
            return carry

        lax.fori_loop(first, last, step, 0)

    barrier = pltpu.get_barrier_semaphore()

    def greet(k):
        pl.semaphore_signal(
            barrier, inc=1, device_id={"wide": other(k)}, device_id_type=pl.DeviceIdType.MESH
        )

    loop(1, n, greet)
    load = pltpu.make_async_copy(ptdf_hbm, ptdf, in_sem)
    load.start()

    for q in range(folds):
        cols = slice(q * span, (q + 1) * span)
        fold_yf[q * hr : (q + 1) * hr, :] = yf_ref[:, cols]
        fold_lim[q * hr : (q + 1) * hr, :] = jnp.broadcast_to(llim_ref[:, cols], (hr, span))

    def own_rows(c, ch):
        return pl.ds(pl.multiple_of((c * nc + ch) * rows, rows), rows)

    duals[0, own_rows(core, chip), :] = fold_yf[...].astype(BF16)

    zone = zone_ref[...]
    member = (iota((n, gens), 0) == zone).astype(F32)
    earlier = (iota((gens, gens), 0) < iota((gens, gens), 1)).astype(F32)
    ahead = dot(member.astype(BF16), earlier.astype(BF16))
    rank = jnp.sum(ahead * member, axis=0, keepdims=True).astype(jnp.int32)
    lanes = payload.shape[1]
    slot_of = jnp.concatenate(
        [zone * cap + rank, jnp.full((1, lanes - gens), -1, jnp.int32)], axis=1
    )
    packing = (iota((slots, lanes), 0) == slot_of).astype(F32)

    payload[...] = jnp.zeros_like(payload)
    payload[0:hours, 0:gens] = cost_ref[...]
    payload[hours : 2 * hours, 0:gens] = x_ref[...]
    payload[2 * hours : 3 * hours, 0:gens] = yr_ref[...]
    payload[3 * hours : 3 * hours + 1, 0:gens] = gmax_ref[...]
    payload[3 * hours + 1 : 3 * hours + 2, 0:gens] = rlim_ref[...]
    payload[3 * hours + 2 : 3 * hours + 3, 0:gens] = local_ref[...].astype(F32) + 1.0
    packed[...] = dot(packing, payload[...], ((1,), (1,)), HIGH)

    pl.semaphore_wait(barrier, n - 1)

    def gather(it):
        mine = duals.at[it, own_rows(core, chip)]
        near = remote(mine, mine, f_send.at[it, 0], f_recv.at[it, 0], partner)
        near.start()

        def out(k):
            return remote(
                mine, mine, g_send.at[it, k], g_recv.at[it, k], chip_after(k) * 2 + core
            )

        loop(1, nc, lambda k: out(k).start())

    def gather_end(it):
        def into(k, c):
            return duals.at[it, own_rows(c, chip_before(k))]

        def forward(k):
            got = into(k, core)
            remote(got, got, g_send.at[it, k], g_recv.at[it, k], partner).wait_recv()
            remote(got, got, f_send.at[it, k], f_recv.at[it, k], partner).start()

        loop(1, nc, forward)

        def finish(k):
            got = into(k, 1 - core)
            remote(got, got, f_send.at[it, k], f_recv.at[it, k], partner).wait_recv()

        loop(0, nc, finish)

    def gather_sent(it):
        mine = duals.at[it, own_rows(core, chip)]
        remote(mine, mine, f_send.at[it, 0], f_recv.at[it, 0], partner).wait_send()

        def sent(k):
            remote(mine, mine, g_send.at[it, k], g_recv.at[it, k], partner).wait_send()
            got = duals.at[it, own_rows(core, chip_before(k))]
            remote(got, got, f_send.at[it, k], f_recv.at[it, k], partner).wait_send()

        loop(1, nc, sent)

    def rows_of(w):
        return pl.ds(pl.multiple_of(w * cap, cap), cap)

    def exchange(src, dst, send, recv):
        def go(k):
            remote(
                src.at[rows_of(other(k))], dst.at[rows_of(me)], send.at[k], recv.at[k], other(k)
            ).start()

        loop(1, n, go)
        dst[rows_of(me), :] = src[rows_of(me), :]

    def exchange_end(src, dst, send, recv):
        def end(k):
            remote(
                src.at[rows_of(other(k))],
                dst.at[rows_of(before(k))],
                send.at[k],
                recv.at[k],
                other(k),
            ).wait()

        loop(1, n, end)

    exchange(packed, arrived, a_send, a_recv)
    gather(0)
    exchange_end(packed, arrived, a_send, a_recv)

    ids = arrived[:, 3 * hours + 2 : 3 * hours + 3].astype(jnp.int32)
    turned[...] = arrived[...].T
    cost = turned[0:hours, :]
    x = turned[hours : 2 * hours, :]
    yr = turned[2 * hours : 3 * hours, :]
    gmax = turned[3 * hours : 3 * hours + 1, :]
    rlim = turned[3 * hours + 1 : 3 * hours + 2, :]
    id_row = turned[3 * hours + 2 : 3 * hours + 3, :].astype(jnp.int32)
    at_bus = (iota((slots, buses), 1) + 1 == ids).astype(F32)
    same_bool = (ids == id_row) & (ids > 0)
    same = same_bool.astype(F32)
    repeats = jnp.max(
        jnp.where(iota((slots, slots), 0) < iota((slots, slots), 1), same, 0.0),
        axis=0,
        keepdims=True,
    )
    lead = jnp.where((repeats == 0.0) & (id_row > 0), 1.0, 0.0)
    yb_slot = dot(at_bus, yb_ref[...].T, precision=HIGH).T
    demand_slot = dot(at_bus, demand_ref[...].T, precision=HIGH).T
    load.wait()
    at_bus16 = at_bus.astype(BF16)
    rows16 = [
        dot(at_bus16, ptdf[:, q * span : (q + 1) * span]).astype(BF16) for q in range(folds)
    ]

    piece_row = iota((n * rows, hours), 0)
    block = piece_row // rows
    owner = lax.rem(block, nc) * 2 + block // nc
    within = lax.rem(piece_row, rows)
    hour_of = owner * hr + lax.rem(within, hr)
    fold_of = within // hr
    at_hour = hour_of == iota((n * rows, hours), 1)
    spread = [(at_hour & (fold_of == q)).astype(F32).astype(BF16) for q in range(folds)]
    t_row = iota((hours, n * rows), 1)
    t_block = t_row // rows
    t_owner = lax.rem(t_block, nc) * 2 + t_block // nc
    t_within = lax.rem(t_row, rows)
    t_at = (t_owner * hr + lax.rem(t_within, hr)) == iota((hours, n * rows), 0)
    collect = [(t_at & (t_within // hr == q)).astype(F32).astype(BF16) for q in range(folds)]

    hour = iota((hours, slots), 0)
    total = jnp.zeros((hours, slots), F32)
    for it in range(ITERS):
        gather_end(it)
        gen_dual = yb_slot
        for q in range(folds):
            line16 = dot(collect[q], duals[it]).astype(BF16)
            gen_dual = gen_dual + dot(line16, rows16[q], ((1,), (1,)))
        masked = jnp.where(hour > 0, yr, 0.0)
        following = jnp.where(hour < hours - 1, pltpu.roll(masked, hours - 1, 0), 0.0)
        moved = x - STEP * (cost + gen_dual + (masked - following))
        x_new = jnp.clip(moved, 0.0, gmax)
        extra = 2.0 * x_new - x
        injection = dot(extra, same, precision=HIGH)
        inj16 = (injection * lead).astype(BF16)
        mixed = None
        for q in range(folds):
            term = dot(dot(spread[q], inj16).astype(BF16), rows16[q])
            mixed = term if mixed is None else mixed + term
        part[it] = mixed

        def give(k):
            return remote(
                part.at[it, own_rows(1 - core, chip_after(k))],
                cbuf.at[it, k],
                c_send.at[it, k],
                c_recv.at[it, k],
                partner,
            )

        def spoke(k):
            return remote(
                sbuf.at[it, k],
                rbuf.at[it, k],
                r_send.at[it, k],
                r_recv.at[it, k],
                chip_after(k) * 2 + core,
            )

        loop(1, nc, lambda k: give(k).start())
        give(0).start()

        total = total + injection
        yb_slot = yb_slot + STEP * (injection - demand_slot)
        change = jnp.where(hour > 0, extra - pltpu.roll(extra, 1, 0), 0.0)
        yr = shrink(yr + STEP * change, rlim)
        x = x_new

        def pass_on(k):
            give(k).wait_recv()
            sbuf[it, k] = part[it, own_rows(core, chip_after(k)), :] + cbuf[it, k]
            spoke(k).start()

        loop(1, nc, pass_on)
        give(0).wait_recv()
        mine = part[it, own_rows(core, chip), :] + cbuf[it, 0]
        if it == ITERS - 1:
            back[...] = jnp.concatenate([x, yr], axis=0).T
            exchange(back, returned, b_send, b_recv)
            placed = dot(total * lead, at_bus, precision=HIGH)
            yb_out[...] = yb_ref[...] + STEP * (placed - ITERS * demand_ref[...])

        def add(k, acc):
            spoke(k).wait_recv()
            return acc + rbuf[it, k]

        flows = lax.fori_loop(1, nc, add, mine)
        fold_yf[...] = shrink(fold_yf[...] + STEP * flows, fold_lim[...])
        if it < ITERS - 1:
            duals[it + 1, own_rows(core, chip), :] = fold_yf[...].astype(BF16)
            gather(it + 1)

    for q in range(folds):
        yf_out[:, q * span : (q + 1) * span] = fold_yf[q * hr : (q + 1) * hr, :]
    exchange_end(back, returned, b_send, b_recv)
    result = dot(returned[...].T, packing, precision=HIGH)
    x_out[...] = result[0:hours, 0:gens]
    yr_out[...] = result[hours : 2 * hours, 0:gens]

    for it in range(ITERS):
        gather_sent(it)

        def done(k):
            remote(
                part.at[it, own_rows(1 - core, chip_after(k))],
                cbuf.at[it, k],
                c_send.at[it, k],
                c_recv.at[it, k],
                partner,
            ).wait_send()

        loop(0, nc, done)

        def done_far(k):
            remote(
                sbuf.at[it, k], rbuf.at[it, k], r_send.at[it, k], r_recv.at[it, k], partner
            ).wait_send()

        loop(1, nc, done_far)


def hand_on(*refs):
    sems = refs[8]
    copies = [pltpu.make_async_copy(refs[i], refs[4 + i], sems.at[i]) for i in range(4)]
    for copy in copies:
        copy.start()
    for copy in copies:
        copy.wait()


def per_device(
    gen_cost,
    demand,
    ptdf_rows,
    gen_zone,
    gen_local,
    gen_max,
    ramp_limit,
    line_limit,
    primal_start,
    balance_start,
    flow_start,
    ramp_start,
):
    n = lax.axis_size("wide")
    nc = n // 2
    gens, hours = primal_start.shape
    buses, lines = ptdf_rows.shape
    hr = flow_start.shape[0]
    cap = -(-max(2, 2 * gens // n) // 8) * 8
    slots = n * cap
    folds = max(1, 16 // hr)
    rows = hr * folds
    span = lines // folds
    width = -(-(3 * hours + 3) // 128) * 128
    vmem = pl.BlockSpec(memory_space=pltpu.VMEM)
    dma = pltpu.SemaphoreType.DMA
    shape = jax.ShapeDtypeStruct
    results = pl.pallas_call(
        functools.partial(kernel, n, cap),
        out_shape=(
            shape((hours, gens), F32),
            shape((hours, buses), F32),
            shape(flow_start.shape, F32),
            shape((hours, gens), F32),
        ),
        in_specs=[vmem, vmem, pl.BlockSpec(memory_space=pl.ANY)] + [vmem] * 9,
        out_specs=(vmem,) * 4,
        scratch_shapes=[
            pltpu.VMEM((buses, lines), BF16),
            pltpu.VMEM((width, -(-gens // 128) * 128), F32),
            pltpu.VMEM((slots, width), F32),
            pltpu.VMEM((slots, width), F32),
            pltpu.VMEM((width, slots), F32),
            pltpu.VMEM((slots, 2 * hours), F32),
            pltpu.VMEM((slots, 2 * hours), F32),
            pltpu.VMEM((ITERS, n * rows, span), F32),
            pltpu.VMEM((ITERS, nc, rows, span), F32),
            pltpu.VMEM((ITERS, nc, rows, span), F32),
            pltpu.VMEM((ITERS, nc, rows, span), F32),
            pltpu.VMEM((ITERS, n * rows, span), BF16),
            pltpu.VMEM((rows, span), F32),
            pltpu.VMEM((rows, span), F32),
            dma(()),
            dma((n,)),
            dma((n,)),
            dma((n,)),
            dma((n,)),
        ]
        + [dma((ITERS, nc))] * 8,
        compiler_params=pltpu.CompilerParams(
            collective_id=0, has_side_effects=True, vmem_limit_bytes=56 * 1024 * 1024
        ),
    )(
        gen_cost.T,
        demand.T,
        ptdf_rows,
        gen_zone.reshape(1, gens),
        gen_local.reshape(1, gens),
        gen_max.reshape(1, gens),
        ramp_limit.reshape(1, gens),
        line_limit.reshape(1, lines),
        primal_start.T,
        balance_start.T,
        flow_start,
        ramp_start.T,
    )
    anywhere = pl.BlockSpec(memory_space=pltpu.HBM)
    primal, balance, flow, ramp = pl.pallas_call(
        hand_on,
        out_shape=tuple(shape(r.shape, F32) for r in results),
        in_specs=[anywhere] * 4,
        out_specs=(anywhere,) * 4,
        scratch_shapes=[dma((4,))],
    )(*results)
    return primal.T, balance.T, flow, ramp.T


def solution(mesh):
    both = P(("groups", "wide"), None)
    placed = (
        both,
        both,
        P("wide", None),
        P("wide", None),
        P("wide"),
        P("wide"),
        P("wide"),
        P(),
        both,
        both,
        both,
        both,
    )
    return jax.shard_map(
        per_device, mesh=mesh, in_specs=placed, out_specs=(both,) * 4, check_vma=False
    )
```

```python
import functools

import jax
import jax.numpy as jnp
from jax import lax
from jax.experimental import pallas as pl
from jax.experimental.pallas import tpu as pltpu
from jax.sharding import PartitionSpec as P

ITERS = 3
STEP = 0.25
F32 = jnp.float32
BF16 = jnp.bfloat16
HIGH = lax.Precision.HIGHEST


def dot(a, b, dims=((1,), (0,)), precision=None):
    return lax.dot_general(a, b, (dims, ((), ())), preferred_element_type=F32, precision=precision)


def iota(shape, dim):
    return lax.broadcasted_iota(jnp.int32, shape, dim)


def shrink(value, limit):
    return value - STEP * jnp.clip(value * (1.0 / STEP), -limit, limit)


def kernel(
    n,
    cap,
    cost_ref,
    demand_ref,
    ptdf_hbm,
    zone_ref,
    local_ref,
    gmax_ref,
    rlim_ref,
    llim_ref,
    x_ref,
    yb_ref,
    yf_ref,
    yr_ref,
    x_out,
    yb_out,
    yf_out,
    yr_out,
    ptdf,
    payload,
    packed,
    arrived,
    turned,
    back,
    returned,
    part,
    cbuf,
    sbuf,
    rbuf,
    duals,
    near_rows,
    state,
    swap_out,
    swap_in,
    in_sem,
    a_send,
    a_recv,
    b_send,
    b_recv,
    c_send,
    c_recv,
    r_send,
    r_recv,
    g_send,
    g_recv,
    f_send,
    f_recv,
    s_send,
    s_recv,
):
    nc = n // 2
    hours, gens = cost_ref.shape
    buses, lines = ptdf.shape
    hr = yf_ref.shape[0]
    slots = n * cap
    tile = 2 * hr
    rows = 2 * tile
    half = lines // 2
    span = half // 2
    me = lax.axis_index("wide")
    core = lax.rem(me, 2)
    chip = me // 2
    partner = chip * 2 + 1 - core

    def other(k):
        return lax.rem(me + k, n)

    def before(k):
        return lax.rem(me + n - k, n)

    def chip_after(k):
        return lax.rem(chip + k, nc)

    def chip_before(k):
        return lax.rem(chip + nc - k, nc)

    def remote(src, dst, send, recv, target):
        return pltpu.make_async_remote_copy(
            src_ref=src,
            dst_ref=dst,
            send_sem=send,
            recv_sem=recv,
            device_id={"wide": target},
            device_id_type=pl.DeviceIdType.MESH,
        )

    def loop(first, last, body):
        def step(k, carry):
            body(k)
            return carry

        lax.fori_loop(first, last, step, 0)

    barrier = pltpu.get_barrier_semaphore()

    def greet(k):
        pl.semaphore_signal(
            barrier, inc=1, device_id={"wide": other(k)}, device_id_type=pl.DeviceIdType.MESH
        )

    loop(1, n, greet)
    load = pltpu.make_async_copy(ptdf_hbm, ptdf, in_sem)
    load.start()

    def own_rows(c, ch):
        return pl.ds(pl.multiple_of((c * nc + ch) * rows, rows), rows)

    def hours_of(ch):
        return pl.ds(pl.multiple_of(ch * tile, tile), tile)

    def pick(first, second):
        return jnp.where(core == 0, first, second)

    def swap(i):
        return remote(swap_out.at[i], swap_in.at[i], s_send.at[i], s_recv.at[i], partner)

    def keep_rounded(it):
        now = state[...]
        duals[it, own_rows(core, chip), :] = jnp.concatenate(
            [now[:, :span], now[:, span:]], axis=0
        ).astype(BF16)

    limit = pick(llim_ref[:, :half], llim_ref[:, half:])
    swap_out[0] = pick(yf_ref[:, half:], yf_ref[:, :half])

    zone = zone_ref[...]
    member = (iota((n, gens), 0) == zone).astype(F32)
    earlier = (iota((gens, gens), 0) < iota((gens, gens), 1)).astype(F32)
    ahead = dot(member.astype(BF16), earlier.astype(BF16))
    rank = jnp.sum(ahead * member, axis=0, keepdims=True).astype(jnp.int32)
    lanes = payload.shape[1]
    slot_of = jnp.concatenate(
        [zone * cap + rank, jnp.full((1, lanes - gens), -1, jnp.int32)], axis=1
    )
    packing = (iota((slots, lanes), 0) == slot_of).astype(F32)

    payload[...] = jnp.zeros_like(payload)
    payload[0:hours, 0:gens] = cost_ref[...]
    payload[hours : 2 * hours, 0:gens] = x_ref[...]
    payload[2 * hours : 3 * hours, 0:gens] = yr_ref[...]
    payload[3 * hours : 3 * hours + 1, 0:gens] = gmax_ref[...]
    payload[3 * hours + 1 : 3 * hours + 2, 0:gens] = rlim_ref[...]
    payload[3 * hours + 2 : 3 * hours + 3, 0:gens] = local_ref[...].astype(F32) + 1.0
    packed[...] = dot(packing, payload[...], ((1,), (1,)), HIGH)

    pl.semaphore_wait(barrier, n - 1)

    def gather(it):
        mine = duals.at[it, own_rows(core, chip)]
        near = remote(mine, mine, f_send.at[it, 0], f_recv.at[it, 0], partner)
        near.start()

        def out(k):
            return remote(
                mine, mine, g_send.at[it, k], g_recv.at[it, k], chip_after(k) * 2 + core
            )

        loop(1, nc, lambda k: out(k).start())

    def gather_far(it):
        def forward(k):
            got = duals.at[it, own_rows(core, chip_before(k))]
            remote(got, got, g_send.at[it, k], g_recv.at[it, k], partner).wait_recv()
            remote(got, got, f_send.at[it, k], f_recv.at[it, k], partner).start()

        loop(1, nc, forward)

    def gather_near(it):
        def finish(k):
            got = duals.at[it, own_rows(1 - core, chip_before(k))]
            remote(got, got, f_send.at[it, k], f_recv.at[it, k], partner).wait_recv()

        loop(0, nc, finish)

    def gather_sent(it):
        mine = duals.at[it, own_rows(core, chip)]
        remote(mine, mine, f_send.at[it, 0], f_recv.at[it, 0], partner).wait_send()

        def sent(k):
            remote(mine, mine, g_send.at[it, k], g_recv.at[it, k], partner).wait_send()
            got = duals.at[it, own_rows(core, chip_before(k))]
            remote(got, got, f_send.at[it, k], f_recv.at[it, k], partner).wait_send()

        loop(1, nc, sent)

    def rows_of(w):
        return pl.ds(pl.multiple_of(w * cap, cap), cap)

    def exchange(src, dst, send, recv):
        def go(k):
            remote(
                src.at[rows_of(other(k))], dst.at[rows_of(me)], send.at[k], recv.at[k], other(k)
            ).start()

        loop(1, n, go)
        dst[rows_of(me), :] = src[rows_of(me), :]

    def exchange_end(src, dst, send, recv):
        def end(k):
            remote(
                src.at[rows_of(other(k))],
                dst.at[rows_of(before(k))],
                send.at[k],
                recv.at[k],
                other(k),
            ).wait()

        loop(1, n, end)

    swap(0).start()
    exchange(packed, arrived, a_send, a_recv)
    swap(0).wait()
    held = pick(yf_ref[:, :half], yf_ref[:, half:])
    state[0:hr, :] = pick(held, swap_in[0])
    state[hr:tile, :] = pick(swap_in[0], held)
    keep_rounded(0)
    gather(0)
    exchange_end(packed, arrived, a_send, a_recv)

    ids = arrived[:, 3 * hours + 2 : 3 * hours + 3].astype(jnp.int32)
    turned[...] = arrived[...].T
    cost = turned[0:hours, :]
    x = turned[hours : 2 * hours, :]
    yr = turned[2 * hours : 3 * hours, :]
    gmax = turned[3 * hours : 3 * hours + 1, :]
    rlim = turned[3 * hours + 1 : 3 * hours + 2, :]
    id_row = turned[3 * hours + 2 : 3 * hours + 3, :].astype(jnp.int32)
    at_bus = (iota((slots, buses), 1) + 1 == ids).astype(F32)
    same_bool = (ids == id_row) & (ids > 0)
    same = same_bool.astype(F32)
    repeats = jnp.max(
        jnp.where(iota((slots, slots), 0) < iota((slots, slots), 1), same, 0.0),
        axis=0,
        keepdims=True,
    )
    lead = jnp.where((repeats == 0.0) & (id_row > 0), 1.0, 0.0)
    bus_rows = jnp.concatenate([yb_ref[...], demand_ref[...]], axis=0).T
    slot_rows = dot(at_bus, bus_rows, precision=HIGH).T
    yb_slot = slot_rows[0:hours, :]
    demand_slot = slot_rows[hours : 2 * hours, :]
    load.wait()
    at_bus16 = at_bus.astype(BF16)
    for c in range(2):
        near_rows[c] = dot(at_bus16, ptdf[:, c * half : (c + 1) * half]).astype(BF16)

    def prices(it, c):
        got = duals[it, pl.ds(pl.multiple_of(c * nc * rows, nc * rows), nc * rows), :]
        got = got.astype(F32).reshape(nc, 2, tile, span)
        sums = None
        for u in range(2):
            line16 = got[:, u].reshape(hours, span).astype(BF16)
            term = dot(line16, near_rows[c, :, u * span : (u + 1) * span], ((1,), (1,)))
            sums = term if sums is None else sums + term
        return sums

    hour = iota((hours, slots), 0)
    total = jnp.zeros((hours, slots), F32)
    for it in range(ITERS):
        gather_far(it)
        gen_dual = yb_slot + prices(it, core)
        gather_near(it)
        gen_dual = gen_dual + prices(it, 1 - core)
        masked = jnp.where(hour > 0, yr, 0.0)
        following = jnp.where(hour < hours - 1, pltpu.roll(masked, hours - 1, 0), 0.0)
        moved = x - STEP * (cost + gen_dual + (masked - following))
        x_new = jnp.clip(moved, 0.0, gmax)
        extra = 2.0 * x_new - x
        injection = dot(extra, same, precision=HIGH)
        inj16 = (injection * lead).astype(BF16)
        part[it, 1 - core] = dot(inj16, near_rows[1 - core])

        def give(k):
            return remote(
                part.at[it, 1 - core, hours_of(chip_after(k))],
                cbuf.at[it, k],
                c_send.at[it, k],
                c_recv.at[it, k],
                partner,
            )

        def spoke(k):
            return remote(
                sbuf.at[it, k],
                rbuf.at[it, k],
                r_send.at[it, k],
                r_recv.at[it, k],
                chip_after(k) * 2 + core,
            )

        loop(1, nc, lambda k: give(k).start())
        give(0).start()
        part[it, core] = dot(inj16, near_rows[core])

        def pass_on(k):
            give(k).wait_recv()
            sbuf[it, k] = part[it, core, hours_of(chip_after(k)), :] + cbuf[it, k]
            spoke(k).start()

        loop(1, nc, pass_on)
        give(0).wait_recv()
        mine = part[it, core, hours_of(chip), :] + cbuf[it, 0]

        total = total + injection
        yb_slot = yb_slot + STEP * (injection - demand_slot)
        change = jnp.where(hour > 0, extra - pltpu.roll(extra, 1, 0), 0.0)
        yr = shrink(yr + STEP * change, rlim)
        x = x_new
        if it == ITERS - 1:
            back[...] = jnp.concatenate([x, yr], axis=0).T
            exchange(back, returned, b_send, b_recv)
            placed = dot(total * lead, at_bus, precision=HIGH)
            yb_out[...] = yb_ref[...] + STEP * (placed - ITERS * demand_ref[...])

        def add(k, acc):
            spoke(k).wait_recv()
            return acc + rbuf[it, k]

        flows = lax.fori_loop(1, nc, add, mine)
        state[...] = shrink(state[...] + STEP * flows, limit)
        if it < ITERS - 1:
            keep_rounded(it + 1)
            gather(it + 1)

    swap_out[1] = pick(state[hr:tile, :], state[0:hr, :])
    swap(1).start()
    exchange_end(back, returned, b_send, b_recv)
    result = dot(returned[...].T, packing, precision=HIGH)
    x_out[...] = result[0:hours, 0:gens]
    yr_out[...] = result[hours : 2 * hours, 0:gens]

    swap(1).wait()
    held = pick(state[0:hr, :], state[hr:tile, :])
    yf_out[:, :half] = pick(held, swap_in[1])
    yf_out[:, half:] = pick(swap_in[1], held)

    for it in range(ITERS):
        gather_sent(it)

        def done(k):
            remote(
                part.at[it, 1 - core, hours_of(chip_after(k))],
                cbuf.at[it, k],
                c_send.at[it, k],
                c_recv.at[it, k],
                partner,
            ).wait_send()

        loop(0, nc, done)

        def done_far(k):
            remote(
                sbuf.at[it, k], rbuf.at[it, k], r_send.at[it, k], r_recv.at[it, k], partner
            ).wait_send()

        loop(1, nc, done_far)


def hand_on(*refs):
    for i in range(4):
        refs[4 + i][...] = refs[i][...]


def per_device(
    gen_cost,
    demand,
    ptdf_rows,
    gen_zone,
    gen_local,
    gen_max,
    ramp_limit,
    line_limit,
    primal_start,
    balance_start,
    flow_start,
    ramp_start,
):
    n = lax.axis_size("wide")
    nc = n // 2
    gens, hours = primal_start.shape
    buses, lines = ptdf_rows.shape
    hr = flow_start.shape[0]
    cap = -(-max(2, 2 * gens // n) // 8) * 8
    slots = n * cap
    tile = 2 * hr
    half = lines // 2
    width = -(-(3 * hours + 3) // 128) * 128
    vmem = pl.BlockSpec(memory_space=pltpu.VMEM)
    dma = pltpu.SemaphoreType.DMA
    shape = jax.ShapeDtypeStruct
    results = pl.pallas_call(
        functools.partial(kernel, n, cap),
        out_shape=(
            shape((hours, gens), F32),
            shape((hours, buses), F32),
            shape(flow_start.shape, F32),
            shape((hours, gens), F32),
        ),
        in_specs=[vmem, vmem, pl.BlockSpec(memory_space=pl.ANY)] + [vmem] * 9,
        out_specs=(vmem,) * 4,
        scratch_shapes=[
            pltpu.VMEM((buses, lines), BF16),
            pltpu.VMEM((width, -(-gens // 128) * 128), F32),
            pltpu.VMEM((slots, width), F32),
            pltpu.VMEM((slots, width), F32),
            pltpu.VMEM((width, slots), F32),
            pltpu.VMEM((slots, 2 * hours), F32),
            pltpu.VMEM((slots, 2 * hours), F32),
            pltpu.VMEM((ITERS, 2, hours, half), F32),
            pltpu.VMEM((ITERS, nc, tile, half), F32),
            pltpu.VMEM((ITERS, nc, tile, half), F32),
            pltpu.VMEM((ITERS, nc, tile, half), F32),
            pltpu.VMEM((ITERS, n * 2 * tile, half // 2), BF16),
            pltpu.VMEM((2, slots, half), BF16),
            pltpu.VMEM((tile, half), F32),
            pltpu.VMEM((2, hr, half), F32),
            pltpu.VMEM((2, hr, half), F32),
            dma(()),
            dma((n,)),
            dma((n,)),
            dma((n,)),
            dma((n,)),
        ]
        + [dma((ITERS, nc))] * 8
        + [dma((2,))] * 2,
        compiler_params=pltpu.CompilerParams(
            collective_id=0, has_side_effects=True, vmem_limit_bytes=56 * 1024 * 1024
        ),
    )(
        gen_cost.T,
        demand.T,
        ptdf_rows,
        gen_zone.reshape(1, gens),
        gen_local.reshape(1, gens),
        gen_max.reshape(1, gens),
        ramp_limit.reshape(1, gens),
        line_limit.reshape(1, lines),
        primal_start.T,
        balance_start.T,
        flow_start,
        ramp_start.T,
    )
    primal, balance, flow, ramp = pl.pallas_call(
        hand_on,
        out_shape=tuple(shape(r.shape, F32) for r in results),
        in_specs=[vmem] * 4,
        out_specs=(vmem,) * 4,
    )(*results)
    return primal.T, balance.T, flow, ramp.T


def solution(mesh):
    both = P(("groups", "wide"), None)
    placed = (
        both,
        both,
        P("wide", None),
        P("wide", None),
        P("wide"),
        P("wide"),
        P("wide"),
        P(),
        both,
        both,
        both,
        both,
    )
    return jax.shard_map(
        per_device, mesh=mesh, in_specs=placed, out_specs=(both,) * 4, check_vma=False
    )
```

```python
import functools

import jax
import jax.numpy as jnp
from jax import lax
from jax.experimental import pallas as pl
from jax.experimental.pallas import tpu as pltpu
from jax.sharding import PartitionSpec as P

ITERS = 3
STEP = 0.25
F32 = jnp.float32
BF16 = jnp.bfloat16
HIGH = lax.Precision.HIGHEST


def dot(a, b, dims=((1,), (0,)), precision=None):
    return lax.dot_general(a, b, (dims, ((), ())), preferred_element_type=F32, precision=precision)


def iota(shape, dim):
    return lax.broadcasted_iota(jnp.int32, shape, dim)


def shrink(value, limit):
    return value - STEP * jnp.clip(value * (1.0 / STEP), -limit, limit)


def kernel(
    n,
    cap,
    cost_ref,
    demand_ref,
    ptdf_hbm,
    zone_ref,
    local_ref,
    gmax_ref,
    rlim_ref,
    llim_ref,
    x_ref,
    yb_ref,
    yf_ref,
    yr_ref,
    x_out,
    yb_out,
    yf_out,
    yr_out,
    ptdf,
    payload,
    packed,
    arrived,
    turned,
    back,
    returned,
    part,
    cbuf,
    sbuf,
    rbuf,
    duals,
    near_rows,
    state,
    swap_out,
    swap_in,
    in_sem,
    a_send,
    a_recv,
    b_send,
    b_recv,
    c_send,
    c_recv,
    r_send,
    r_recv,
    g_send,
    g_recv,
    f_send,
    f_recv,
    s_send,
    s_recv,
):
    nc = n // 2
    hours, gens = cost_ref.shape
    buses, lines = ptdf.shape
    hr = yf_ref.shape[0]
    slots = n * cap
    tile = 2 * hr
    rows = 2 * tile
    half = lines // 2
    span = half // 2
    me = lax.axis_index("wide")
    core = lax.rem(me, 2)
    chip = me // 2
    partner = chip * 2 + 1 - core

    def other(k):
        return lax.rem(me + k, n)

    def before(k):
        return lax.rem(me + n - k, n)

    pairs = nc // 2
    pair, side = chip // 2, lax.rem(chip, 2)

    def chip_of(i):
        to = i // pairs
        where = to * side + (1 - to) * (1 - side)
        return lax.rem(pair + lax.rem(i + 1, pairs), pairs) * 2 + where

    def chip_after(k):
        return lax.rem(chip + k, nc)

    def chip_before(k):
        return lax.rem(chip + nc - k, nc)

    def remote(src, dst, send, recv, target):
        return pltpu.make_async_remote_copy(
            src_ref=src,
            dst_ref=dst,
            send_sem=send,
            recv_sem=recv,
            device_id={"wide": target},
            device_id_type=pl.DeviceIdType.MESH,
        )

    def loop(first, last, body):
        def step(k, carry):
            body(k)
            return carry

        lax.fori_loop(first, last, step, 0)

    barrier = pltpu.get_barrier_semaphore()

    def greet(k):
        pl.semaphore_signal(
            barrier, inc=1, device_id={"wide": other(k)}, device_id_type=pl.DeviceIdType.MESH
        )

    loop(1, n, greet)
    load = pltpu.make_async_copy(ptdf_hbm, ptdf, in_sem)
    load.start()

    def own_rows(c, ch):
        return pl.ds(pl.multiple_of((c * nc + ch) * rows, rows), rows)

    def hours_of(ch):
        return pl.ds(pl.multiple_of(ch * tile, tile), tile)

    def pick(first, second):
        return jnp.where(core == 0, first, second)

    def swap(i):
        return remote(swap_out.at[i], swap_in.at[i], s_send.at[i], s_recv.at[i], partner)

    def keep_rounded(it):
        now = state[...]
        duals[it, own_rows(core, chip), :] = jnp.concatenate(
            [now[:, :span], now[:, span:]], axis=0
        ).astype(BF16)

    limit = pick(llim_ref[:, :half], llim_ref[:, half:])
    swap_out[0] = pick(yf_ref[:, half:], yf_ref[:, :half])

    zone = zone_ref[...]
    member = (iota((n, gens), 0) == zone).astype(F32)
    earlier = (iota((gens, gens), 0) < iota((gens, gens), 1)).astype(F32)
    ahead = dot(member.astype(BF16), earlier.astype(BF16))
    rank = jnp.sum(ahead * member, axis=0, keepdims=True).astype(jnp.int32)
    lanes = payload.shape[1]
    slot_of = jnp.concatenate(
        [zone * cap + rank, jnp.full((1, lanes - gens), -1, jnp.int32)], axis=1
    )
    packing = (iota((slots, lanes), 0) == slot_of).astype(F32)

    payload[...] = jnp.zeros_like(payload)
    payload[0:hours, 0:gens] = cost_ref[...]
    payload[hours : 2 * hours, 0:gens] = x_ref[...]
    payload[2 * hours : 3 * hours, 0:gens] = yr_ref[...]
    payload[3 * hours : 3 * hours + 1, 0:gens] = gmax_ref[...]
    payload[3 * hours + 1 : 3 * hours + 2, 0:gens] = rlim_ref[...]
    payload[3 * hours + 2 : 3 * hours + 3, 0:gens] = local_ref[...].astype(F32) + 1.0
    packed[...] = dot(packing, payload[...], ((1,), (1,)), HIGH)

    pl.semaphore_wait(barrier, n - 1)

    def gather(it):
        mine = duals.at[it, own_rows(core, chip)]
        near = remote(mine, mine, f_send.at[it, 0], f_recv.at[it, 0], partner)
        near.start()

        def out(k):
            return remote(
                mine, mine, g_send.at[it, k], g_recv.at[it, k], chip_after(k) * 2 + core
            )

        loop(1, nc, lambda k: out(k).start())

    def gather_far(it):
        def forward(k):
            got = duals.at[it, own_rows(core, chip_before(k))]
            remote(got, got, g_send.at[it, k], g_recv.at[it, k], partner).wait_recv()
            remote(got, got, f_send.at[it, k], f_recv.at[it, k], partner).start()

        loop(1, nc, forward)

    def gather_near(it):
        def finish(k):
            got = duals.at[it, own_rows(1 - core, chip_before(k))]
            remote(got, got, f_send.at[it, k], f_recv.at[it, k], partner).wait_recv()

        loop(0, nc, finish)

    def gather_sent(it):
        mine = duals.at[it, own_rows(core, chip)]
        remote(mine, mine, f_send.at[it, 0], f_recv.at[it, 0], partner).wait_send()

        def sent(k):
            remote(mine, mine, g_send.at[it, k], g_recv.at[it, k], partner).wait_send()
            got = duals.at[it, own_rows(core, chip_before(k))]
            remote(got, got, f_send.at[it, k], f_recv.at[it, k], partner).wait_send()

        loop(1, nc, sent)

    def rows_of(w):
        return pl.ds(pl.multiple_of(w * cap, cap), cap)

    def exchange(src, dst, send, recv):
        def go(k):
            remote(
                src.at[rows_of(other(k))], dst.at[rows_of(me)], send.at[k], recv.at[k], other(k)
            ).start()

        loop(1, n, go)
        dst[rows_of(me), :] = src[rows_of(me), :]

    def exchange_end(src, dst, send, recv):
        def end(k):
            remote(
                src.at[rows_of(other(k))],
                dst.at[rows_of(before(k))],
                send.at[k],
                recv.at[k],
                other(k),
            ).wait()

        loop(1, n, end)

    swap(0).start()
    exchange(packed, arrived, a_send, a_recv)
    swap(0).wait()
    held = pick(yf_ref[:, :half], yf_ref[:, half:])
    state[0:hr, :] = pick(held, swap_in[0])
    state[hr:tile, :] = pick(swap_in[0], held)
    keep_rounded(0)
    gather(0)
    exchange_end(packed, arrived, a_send, a_recv)
    gather_far(0)

    ids = arrived[:, 3 * hours + 2 : 3 * hours + 3].astype(jnp.int32)
    turned[...] = arrived[...].T
    cost = turned[0:hours, :]
    x = turned[hours : 2 * hours, :]
    yr = turned[2 * hours : 3 * hours, :]
    gmax = turned[3 * hours : 3 * hours + 1, :]
    rlim = turned[3 * hours + 1 : 3 * hours + 2, :]
    id_row = turned[3 * hours + 2 : 3 * hours + 3, :].astype(jnp.int32)
    at_bus = (iota((slots, buses), 1) + 1 == ids).astype(F32)
    same_bool = (ids == id_row) & (ids > 0)
    same = same_bool.astype(F32)
    repeats = jnp.max(
        jnp.where(iota((slots, slots), 0) < iota((slots, slots), 1), same, 0.0),
        axis=0,
        keepdims=True,
    )
    lead = jnp.where((repeats == 0.0) & (id_row > 0), 1.0, 0.0)
    bus_rows = jnp.concatenate([yb_ref[...], demand_ref[...]], axis=0).T
    slot_rows = dot(at_bus, bus_rows, precision=HIGH).T
    yb_slot = slot_rows[0:hours, :]
    demand_slot = slot_rows[hours : 2 * hours, :]
    load.wait()
    at_bus16 = at_bus.astype(BF16)
    for c in range(2):
        near_rows[c] = dot(at_bus16, ptdf[:, c * half : (c + 1) * half]).astype(BF16)

    def prices(it, c):
        got = duals[it, pl.ds(pl.multiple_of(c * nc * rows, nc * rows), nc * rows), :]
        got = got.astype(F32).reshape(nc, 2, tile, span)
        sums = None
        for u in range(2):
            line16 = got[:, u].reshape(hours, span).astype(BF16)
            term = dot(line16, near_rows[c, :, u * span : (u + 1) * span], ((1,), (1,)))
            sums = term if sums is None else sums + term
        return sums

    hour = iota((hours, slots), 0)
    total = jnp.zeros((hours, slots), F32)
    for it in range(ITERS):
        if it > 0:
            gather_far(it)
        gen_dual = yb_slot + prices(it, core)
        gather_near(it)
        gen_dual = gen_dual + prices(it, 1 - core)
        masked = jnp.where(hour > 0, yr, 0.0)
        following = jnp.where(hour < hours - 1, pltpu.roll(masked, hours - 1, 0), 0.0)
        moved = x - STEP * (cost + gen_dual + (masked - following))
        x_new = jnp.clip(moved, 0.0, gmax)
        extra = 2.0 * x_new - x
        injection = dot(extra, same, precision=HIGH)
        inj16 = (injection * lead).astype(BF16)
        part[it, 1 - core] = dot(inj16, near_rows[1 - core])

        def give(k):
            return remote(
                part.at[it, 1 - core, hours_of(chip_of(k))],
                cbuf.at[it, k],
                c_send.at[it, k],
                c_recv.at[it, k],
                partner,
            )

        def spoke(k, target):
            return remote(
                sbuf.at[it, k], rbuf.at[it, k], r_send.at[it, k], r_recv.at[it, k], target
            )

        loop(0, nc, lambda k: give(k).start())
        part[it, core] = dot(inj16, near_rows[core])

        def across(k):
            give(k).wait_recv()
            sbuf[it, k] = part[it, core, hours_of(chip_of(k)), :] + cbuf[it, k]
            spoke(k, (pair * 2 + 1 - side) * 2 + core).start()

        loop(0, pairs, across)

        def along(k):
            give(k).wait_recv()
            spoke(k - pairs, partner).wait_recv()
            own = part[it, core, hours_of(chip_of(k)), :] + cbuf[it, k]
            sbuf[it, k] = own + rbuf[it, k - pairs]
            spoke(k, chip_of(k) * 2 + core).start()

        loop(pairs, nc - 1, along)
        give(nc - 1).wait_recv()
        spoke(pairs - 1, partner).wait_recv()
        mine = part[it, core, hours_of(chip), :] + cbuf[it, nc - 1] + rbuf[it, pairs - 1]

        total = total + injection
        yb_slot = yb_slot + STEP * (injection - demand_slot)
        change = jnp.where(hour > 0, extra - pltpu.roll(extra, 1, 0), 0.0)
        yr = shrink(yr + STEP * change, rlim)
        x = x_new
        if it == ITERS - 1:
            back[...] = jnp.concatenate([x, yr], axis=0).T
            exchange(back, returned, b_send, b_recv)
            placed = dot(total * lead, at_bus, precision=HIGH)
            yb_out[...] = yb_ref[...] + STEP * (placed - ITERS * demand_ref[...])

        def add(k, acc):
            spoke(k, partner).wait_recv()
            return acc + rbuf[it, k]

        flows = lax.fori_loop(pairs, nc - 1, add, mine)
        state[...] = shrink(state[...] + STEP * flows, limit)
        if it < ITERS - 1:
            keep_rounded(it + 1)
            gather(it + 1)

    swap_out[1] = pick(state[hr:tile, :], state[0:hr, :])
    swap(1).start()
    exchange_end(back, returned, b_send, b_recv)
    result = dot(returned[...].T, packing, precision=HIGH)
    x_out[...] = result[0:hours, 0:gens]
    yr_out[...] = result[hours : 2 * hours, 0:gens]

    swap(1).wait()
    held = pick(state[0:hr, :], state[hr:tile, :])
    yf_out[:, :half] = pick(held, swap_in[1])
    yf_out[:, half:] = pick(swap_in[1], held)

    for it in range(ITERS):
        gather_sent(it)

        def done(k):
            remote(
                part.at[it, 1 - core, hours_of(chip_of(k))],
                cbuf.at[it, k],
                c_send.at[it, k],
                c_recv.at[it, k],
                partner,
            ).wait_send()

        loop(0, nc, done)

        def done_far(k):
            remote(
                sbuf.at[it, k], rbuf.at[it, k], r_send.at[it, k], r_recv.at[it, k], partner
            ).wait_send()

        loop(0, nc - 1, done_far)


def hand_on(*refs):
    for i in range(4):
        refs[4 + i][...] = refs[i][...]


def per_device(
    gen_cost,
    demand,
    ptdf_rows,
    gen_zone,
    gen_local,
    gen_max,
    ramp_limit,
    line_limit,
    primal_start,
    balance_start,
    flow_start,
    ramp_start,
):
    n = lax.axis_size("wide")
    nc = n // 2
    gens, hours = primal_start.shape
    buses, lines = ptdf_rows.shape
    hr = flow_start.shape[0]
    cap = -(-max(2, 2 * gens // n) // 8) * 8
    slots = n * cap
    tile = 2 * hr
    half = lines // 2
    width = -(-(3 * hours + 3) // 128) * 128
    vmem = pl.BlockSpec(memory_space=pltpu.VMEM)
    dma = pltpu.SemaphoreType.DMA
    shape = jax.ShapeDtypeStruct
    results = pl.pallas_call(
        functools.partial(kernel, n, cap),
        out_shape=(
            shape((hours, gens), F32),
            shape((hours, buses), F32),
            shape(flow_start.shape, F32),
            shape((hours, gens), F32),
        ),
        in_specs=[vmem, vmem, pl.BlockSpec(memory_space=pl.ANY)] + [vmem] * 9,
        out_specs=(vmem,) * 4,
        scratch_shapes=[
            pltpu.VMEM((buses, lines), BF16),
            pltpu.VMEM((width, -(-gens // 128) * 128), F32),
            pltpu.VMEM((slots, width), F32),
            pltpu.VMEM((slots, width), F32),
            pltpu.VMEM((width, slots), F32),
            pltpu.VMEM((slots, 2 * hours), F32),
            pltpu.VMEM((slots, 2 * hours), F32),
            pltpu.VMEM((ITERS, 2, hours, half), F32),
            pltpu.VMEM((ITERS, nc, tile, half), F32),
            pltpu.VMEM((ITERS, nc, tile, half), F32),
            pltpu.VMEM((ITERS, nc, tile, half), F32),
            pltpu.VMEM((ITERS, n * 2 * tile, half // 2), BF16),
            pltpu.VMEM((2, slots, half), BF16),
            pltpu.VMEM((tile, half), F32),
            pltpu.VMEM((2, hr, half), F32),
            pltpu.VMEM((2, hr, half), F32),
            dma(()),
            dma((n,)),
            dma((n,)),
            dma((n,)),
            dma((n,)),
        ]
        + [dma((ITERS, nc))] * 8
        + [dma((2,))] * 2,
        compiler_params=pltpu.CompilerParams(
            collective_id=0, has_side_effects=True, vmem_limit_bytes=56 * 1024 * 1024
        ),
    )(
        gen_cost.T,
        demand.T,
        ptdf_rows,
        gen_zone.reshape(1, gens),
        gen_local.reshape(1, gens),
        gen_max.reshape(1, gens),
        ramp_limit.reshape(1, gens),
        line_limit.reshape(1, lines),
        primal_start.T,
        balance_start.T,
        flow_start,
        ramp_start.T,
    )
    primal, balance, flow, ramp = pl.pallas_call(
        hand_on,
        out_shape=tuple(shape(r.shape, F32) for r in results),
        in_specs=[vmem] * 4,
        out_specs=(vmem,) * 4,
    )(*results)
    return primal.T, balance.T, flow, ramp.T


def solution(mesh):
    both = P(("groups", "wide"), None)
    placed = (
        both,
        both,
        P("wide", None),
        P("wide", None),
        P("wide"),
        P("wide"),
        P("wide"),
        P(),
        both,
        both,
        both,
        both,
    )
    return jax.shard_map(
        per_device, mesh=mesh, in_specs=placed, out_specs=(both,) * 4, check_vma=False
    )
```

```python
import functools

import jax
import jax.numpy as jnp
from jax import lax
from jax.experimental import pallas as pl
from jax.experimental.pallas import tpu as pltpu
from jax.sharding import PartitionSpec as P

ITERS = 3
STEP = 0.25
F32 = jnp.float32
BF16 = jnp.bfloat16
HIGH = lax.Precision.HIGHEST


def dot(a, b, dims=((1,), (0,)), precision=None):
    return lax.dot_general(a, b, (dims, ((), ())), preferred_element_type=F32, precision=precision)


def iota(shape, dim):
    return lax.broadcasted_iota(jnp.int32, shape, dim)


def shrink(value, limit):
    return value - STEP * jnp.clip(value * (1.0 / STEP), -limit, limit)


def kernel(
    n,
    cap,
    cost_ref,
    demand_ref,
    ptdf_hbm,
    zone_ref,
    local_ref,
    gmax_ref,
    rlim_ref,
    llim_ref,
    x_ref,
    yb_ref,
    yf_ref,
    yr_ref,
    x_out,
    yb_out,
    yf_out,
    yr_out,
    ptdf,
    payload,
    packed,
    arrived,
    packed_ids,
    arrived_ids,
    turned,
    back,
    returned,
    part,
    cbuf,
    sbuf,
    rbuf,
    duals,
    near_rows,
    state,
    swap_out,
    swap_in,
    in_sem,
    a_send,
    a_recv,
    b_send,
    b_recv,
    c_send,
    c_recv,
    r_send,
    r_recv,
    g_send,
    g_recv,
    f_send,
    f_recv,
    s_send,
    s_recv,
    i_send,
    i_recv,
):
    nc = n // 2
    hours, gens = cost_ref.shape
    buses, lines = ptdf.shape
    hr = yf_ref.shape[0]
    slots = n * cap
    tile = 2 * hr
    rows = 2 * tile
    half = lines // 2
    span = half // 2
    me = lax.axis_index("wide")
    core = lax.rem(me, 2)
    chip = me // 2
    partner = chip * 2 + 1 - core

    def other(k):
        return lax.rem(me + k, n)

    def before(k):
        return lax.rem(me + n - k, n)

    def chip_after(k):
        return lax.rem(chip + k, nc)

    def chip_before(k):
        return lax.rem(chip + nc - k, nc)

    def remote(src, dst, send, recv, target):
        return pltpu.make_async_remote_copy(
            src_ref=src,
            dst_ref=dst,
            send_sem=send,
            recv_sem=recv,
            device_id={"wide": target},
            device_id_type=pl.DeviceIdType.MESH,
        )

    def loop(first, last, body):
        def step(k, carry):
            body(k)
            return carry

        lax.fori_loop(first, last, step, 0)

    barrier = pltpu.get_barrier_semaphore()

    def greet(k):
        pl.semaphore_signal(
            barrier, inc=1, device_id={"wide": other(k)}, device_id_type=pl.DeviceIdType.MESH
        )

    loop(1, n, greet)
    load = pltpu.make_async_copy(ptdf_hbm, ptdf, in_sem)
    load.start()

    def own_rows(c, ch):
        return pl.ds(pl.multiple_of((c * nc + ch) * rows, rows), rows)

    def hours_of(ch):
        return pl.ds(pl.multiple_of(ch * tile, tile), tile)

    def pick(first, second):
        return jnp.where(core == 0, first, second)

    def swap(i):
        return remote(swap_out.at[i], swap_in.at[i], s_send.at[i], s_recv.at[i], partner)

    def keep_rounded(it):
        now = state[...]
        duals[it, own_rows(core, chip), :] = jnp.concatenate(
            [now[:, :span], now[:, span:]], axis=0
        ).astype(BF16)

    limit = pick(llim_ref[:, :half], llim_ref[:, half:])
    swap_out[0] = pick(yf_ref[:, half:], yf_ref[:, :half])

    zone = zone_ref[...]
    member = (iota((n, gens), 0) == zone).astype(F32)
    earlier = (iota((gens, gens), 0) < iota((gens, gens), 1)).astype(F32)
    ahead = dot(member.astype(BF16), earlier.astype(BF16))
    rank = jnp.sum(ahead * member, axis=0, keepdims=True).astype(jnp.int32)
    lanes = payload.shape[1]
    slot_of = jnp.concatenate(
        [zone * cap + rank, jnp.full((1, lanes - gens), -1, jnp.int32)], axis=1
    )
    packing = (iota((slots, lanes), 0) == slot_of).astype(F32)

    payload[...] = jnp.zeros_like(payload)
    payload[0:hours, 0:gens] = cost_ref[...]
    payload[hours : 2 * hours, 0:gens] = x_ref[...]
    payload[2 * hours : 3 * hours, 0:gens] = yr_ref[...]
    payload[3 * hours : 3 * hours + 1, 0:gens] = gmax_ref[...]
    payload[3 * hours + 1 : 3 * hours + 2, 0:gens] = rlim_ref[...]
    payload[3 * hours + 2 : 3 * hours + 3, 0:gens] = local_ref[...].astype(F32) + 1.0
    split = packed.shape[1]
    filled = dot(packing, payload[...], ((1,), (1,)), HIGH)
    packed[...] = filled[:, :split]
    packed_ids[...] = filled[:, split:]

    pl.semaphore_wait(barrier, n - 1)

    def gather(it):
        mine = duals.at[it, own_rows(core, chip)]
        near = remote(mine, mine, f_send.at[it, 0], f_recv.at[it, 0], partner)
        near.start()

        def out(k):
            return remote(
                mine, mine, g_send.at[it, k], g_recv.at[it, k], chip_after(k) * 2 + core
            )

        loop(1, nc, lambda k: out(k).start())

    def gather_far(it):
        def forward(k):
            got = duals.at[it, own_rows(core, chip_before(k))]
            remote(got, got, g_send.at[it, k], g_recv.at[it, k], partner).wait_recv()
            remote(got, got, f_send.at[it, k], f_recv.at[it, k], partner).start()

        loop(1, nc, forward)

    def gather_near(it):
        def finish(k):
            got = duals.at[it, own_rows(1 - core, chip_before(k))]
            remote(got, got, f_send.at[it, k], f_recv.at[it, k], partner).wait_recv()

        loop(0, nc, finish)

    def gather_sent(it):
        mine = duals.at[it, own_rows(core, chip)]
        remote(mine, mine, f_send.at[it, 0], f_recv.at[it, 0], partner).wait_send()

        def sent(k):
            remote(mine, mine, g_send.at[it, k], g_recv.at[it, k], partner).wait_send()
            got = duals.at[it, own_rows(core, chip_before(k))]
            remote(got, got, f_send.at[it, k], f_recv.at[it, k], partner).wait_send()

        loop(1, nc, sent)

    def rows_of(w):
        return pl.ds(pl.multiple_of(w * cap, cap), cap)

    def exchange(src, dst, send, recv):
        def go(k):
            remote(
                src.at[rows_of(other(k))], dst.at[rows_of(me)], send.at[k], recv.at[k], other(k)
            ).start()

        loop(1, n, go)
        dst[rows_of(me), :] = src[rows_of(me), :]

    def exchange_end(src, dst, send, recv):
        def end(k):
            remote(
                src.at[rows_of(other(k))],
                dst.at[rows_of(before(k))],
                send.at[k],
                recv.at[k],
                other(k),
            ).wait()

        loop(1, n, end)

    swap(0).start()
    exchange(packed_ids, arrived_ids, i_send, i_recv)
    swap(0).wait()
    held = pick(yf_ref[:, :half], yf_ref[:, half:])
    state[0:hr, :] = pick(held, swap_in[0])
    state[hr:tile, :] = pick(swap_in[0], held)
    keep_rounded(0)
    gather(0)
    exchange(packed, arrived, a_send, a_recv)
    exchange_end(packed_ids, arrived_ids, i_send, i_recv)

    id_column = 3 * hours + 2 - split
    ids = arrived_ids[:, id_column : id_column + 1].astype(jnp.int32)
    turned[split:, :] = arrived_ids[...].T
    id_row = turned[3 * hours + 2 : 3 * hours + 3, :].astype(jnp.int32)
    at_bus = (iota((slots, buses), 1) + 1 == ids).astype(F32)
    same_bool = (ids == id_row) & (ids > 0)
    same = same_bool.astype(F32)
    repeats = jnp.max(
        jnp.where(iota((slots, slots), 0) < iota((slots, slots), 1), same, 0.0),
        axis=0,
        keepdims=True,
    )
    lead = jnp.where((repeats == 0.0) & (id_row > 0), 1.0, 0.0)
    bus_rows = jnp.concatenate([yb_ref[...], demand_ref[...]], axis=0).T
    slot_rows = dot(at_bus, bus_rows, precision=HIGH).T
    yb_slot = slot_rows[0:hours, :]
    demand_slot = slot_rows[hours : 2 * hours, :]
    load.wait()
    at_bus16 = at_bus.astype(BF16)
    for c in range(2):
        near_rows[c] = dot(at_bus16, ptdf[:, c * half : (c + 1) * half]).astype(BF16)

    def prices(it, c):
        got = duals[it, pl.ds(pl.multiple_of(c * nc * rows, nc * rows), nc * rows), :]
        got = got.astype(F32).reshape(nc, 2, tile, span)
        sums = None
        for u in range(2):
            line16 = got[:, u].reshape(hours, span).astype(BF16)
            term = dot(line16, near_rows[c, :, u * span : (u + 1) * span], ((1,), (1,)))
            sums = term if sums is None else sums + term
        return sums

    hour = iota((hours, slots), 0)
    total = jnp.zeros((hours, slots), F32)
    for it in range(ITERS):
        gather_far(it)
        gen_dual = yb_slot + prices(it, core)
        gather_near(it)
        gen_dual = gen_dual + prices(it, 1 - core)
        if it == 0:
            exchange_end(packed, arrived, a_send, a_recv)
            turned[0:split, :] = arrived[...].T
            cost = turned[0:hours, :]
            x = turned[hours : 2 * hours, :]
            yr = turned[2 * hours : 3 * hours, :]
            gmax = turned[3 * hours : 3 * hours + 1, :]
            rlim = turned[3 * hours + 1 : 3 * hours + 2, :]
        masked = jnp.where(hour > 0, yr, 0.0)
        following = jnp.where(hour < hours - 1, pltpu.roll(masked, hours - 1, 0), 0.0)
        moved = x - STEP * (cost + gen_dual + (masked - following))
        x_new = jnp.clip(moved, 0.0, gmax)
        extra = 2.0 * x_new - x
        injection = dot(extra, same, precision=HIGH)
        inj16 = (injection * lead).astype(BF16)
        part[it, 1 - core] = dot(inj16, near_rows[1 - core])

        def give(k):
            return remote(
                part.at[it, 1 - core, hours_of(chip_after(k))],
                cbuf.at[it, k],
                c_send.at[it, k],
                c_recv.at[it, k],
                partner,
            )

        def spoke(k):
            return remote(
                sbuf.at[it, k],
                rbuf.at[it, k],
                r_send.at[it, k],
                r_recv.at[it, k],
                chip_after(k) * 2 + core,
            )

        loop(1, nc, lambda k: give(k).start())
        give(0).start()
        part[it, core] = dot(inj16, near_rows[core])

        def pass_on(k):
            give(k).wait_recv()
            sbuf[it, k] = part[it, core, hours_of(chip_after(k)), :] + cbuf[it, k]
            spoke(k).start()

        loop(1, nc, pass_on)
        give(0).wait_recv()
        mine = part[it, core, hours_of(chip), :] + cbuf[it, 0]

        total = total + injection
        yb_slot = yb_slot + STEP * (injection - demand_slot)
        change = jnp.where(hour > 0, extra - pltpu.roll(extra, 1, 0), 0.0)
        yr = shrink(yr + STEP * change, rlim)
        x = x_new
        if it == ITERS - 1:
            back[...] = jnp.concatenate([x, yr], axis=0).T
            exchange(back, returned, b_send, b_recv)
            placed = dot(total * lead, at_bus, precision=HIGH)
            yb_out[...] = yb_ref[...] + STEP * (placed - ITERS * demand_ref[...])

        def add(k, acc):
            spoke(k).wait_recv()
            return acc + rbuf[it, k]

        flows = lax.fori_loop(1, nc, add, mine)
        state[...] = shrink(state[...] + STEP * flows, limit)
        if it < ITERS - 1:
            keep_rounded(it + 1)
            gather(it + 1)

    swap_out[1] = pick(state[hr:tile, :], state[0:hr, :])
    swap(1).start()
    exchange_end(back, returned, b_send, b_recv)
    result = dot(returned[...].T, packing, precision=HIGH)
    x_out[...] = result[0:hours, 0:gens]
    yr_out[...] = result[hours : 2 * hours, 0:gens]

    swap(1).wait()
    held = pick(state[0:hr, :], state[hr:tile, :])
    yf_out[:, :half] = pick(held, swap_in[1])
    yf_out[:, half:] = pick(swap_in[1], held)

    for it in range(ITERS):
        gather_sent(it)

        def done(k):
            remote(
                part.at[it, 1 - core, hours_of(chip_after(k))],
                cbuf.at[it, k],
                c_send.at[it, k],
                c_recv.at[it, k],
                partner,
            ).wait_send()

        loop(0, nc, done)

        def done_far(k):
            remote(
                sbuf.at[it, k], rbuf.at[it, k], r_send.at[it, k], r_recv.at[it, k], partner
            ).wait_send()

        loop(1, nc, done_far)


def hand_on(*refs):
    for i in range(4):
        refs[4 + i][...] = refs[i][...]


def per_device(
    gen_cost,
    demand,
    ptdf_rows,
    gen_zone,
    gen_local,
    gen_max,
    ramp_limit,
    line_limit,
    primal_start,
    balance_start,
    flow_start,
    ramp_start,
):
    n = lax.axis_size("wide")
    nc = n // 2
    gens, hours = primal_start.shape
    buses, lines = ptdf_rows.shape
    hr = flow_start.shape[0]
    cap = -(-max(2, 2 * gens // n) // 8) * 8
    slots = n * cap
    tile = 2 * hr
    half = lines // 2
    width = -(-(3 * hours + 3) // 128) * 128
    vmem = pl.BlockSpec(memory_space=pltpu.VMEM)
    dma = pltpu.SemaphoreType.DMA
    shape = jax.ShapeDtypeStruct
    results = pl.pallas_call(
        functools.partial(kernel, n, cap),
        out_shape=(
            shape((hours, gens), F32),
            shape((hours, buses), F32),
            shape(flow_start.shape, F32),
            shape((hours, gens), F32),
        ),
        in_specs=[vmem, vmem, pl.BlockSpec(memory_space=pl.ANY)] + [vmem] * 9,
        out_specs=(vmem,) * 4,
        scratch_shapes=[
            pltpu.VMEM((buses, lines), BF16),
            pltpu.VMEM((width, -(-gens // 128) * 128), F32),
            pltpu.VMEM((slots, width - 128), F32),
            pltpu.VMEM((slots, width - 128), F32),
            pltpu.VMEM((slots, 128), F32),
            pltpu.VMEM((slots, 128), F32),
            pltpu.VMEM((width, slots), F32),
            pltpu.VMEM((slots, 2 * hours), F32),
            pltpu.VMEM((slots, 2 * hours), F32),
            pltpu.VMEM((ITERS, 2, hours, half), F32),
            pltpu.VMEM((ITERS, nc, tile, half), F32),
            pltpu.VMEM((ITERS, nc, tile, half), F32),
            pltpu.VMEM((ITERS, nc, tile, half), F32),
            pltpu.VMEM((ITERS, n * 2 * tile, half // 2), BF16),
            pltpu.VMEM((2, slots, half), BF16),
            pltpu.VMEM((tile, half), F32),
            pltpu.VMEM((2, hr, half), F32),
            pltpu.VMEM((2, hr, half), F32),
            dma(()),
            dma((n,)),
            dma((n,)),
            dma((n,)),
            dma((n,)),
        ]
        + [dma((ITERS, nc))] * 8
        + [dma((2,))] * 2
        + [dma((n,))] * 2,
        compiler_params=pltpu.CompilerParams(
            collective_id=0, has_side_effects=True, vmem_limit_bytes=56 * 1024 * 1024
        ),
    )(
        gen_cost.T,
        demand.T,
        ptdf_rows,
        gen_zone.reshape(1, gens),
        gen_local.reshape(1, gens),
        gen_max.reshape(1, gens),
        ramp_limit.reshape(1, gens),
        line_limit.reshape(1, lines),
        primal_start.T,
        balance_start.T,
        flow_start,
        ramp_start.T,
    )
    primal, balance, flow, ramp = pl.pallas_call(
        hand_on,
        out_shape=tuple(shape(r.shape, F32) for r in results),
        in_specs=[vmem] * 4,
        out_specs=(vmem,) * 4,
    )(*results)
    return primal.T, balance.T, flow, ramp.T


def solution(mesh):
    both = P(("groups", "wide"), None)
    placed = (
        both,
        both,
        P("wide", None),
        P("wide", None),
        P("wide"),
        P("wide"),
        P("wide"),
        P(),
        both,
        both,
        both,
        both,
    )
    return jax.shard_map(
        per_device, mesh=mesh, in_specs=placed, out_specs=(both,) * 4, check_vma=False
    )
```
